32 devices in a mesh: mode: 16 (over z, y, core), tile: 2 (over x).
Axes of the slice: x: 2, y: 2, z: 4, core: 2. Of those that a mesh axis runs over, the one named last changes fastest.
Arguments:
- fluid_temp: bfloat16 [1024, 256, 512], P('mode', 'tile'), may hold values from -6 to 6
- solid_temp: float32 [2, 512, 64, 1024], P(None, 'mode', None, 'tile'), may hold values from -6 to 6
- material: int32 [2, 512, 64, 1024], P(None, 'mode', None, 'tile'), may hold values from 0 to 3
Outputs:
- fluid_modes: float32 [1024, 256, 512], P(('mode', 'tile'))
- solid_next: float32 [2, 512, 64, 1024], P(None, 'mode', None, 'tile')
The draws below stay inside these ranges and needn't reach their ends.
All inputs are finite; a program needn't handle non-finite values.
Results may differ from the reference program's by a relative error of at most 0.0003.
Values may be sent and summed in bfloat16 or wider, within the bound.
A program may use at most 192 MiB of HBM per device.

```python
import math
import jax
import jax.numpy as jnp
from jax import lax

NZ = 1024
NY = 256
NX = 512
SY = 64
SUBSTEPS = 4


def with_ends(drawn, key, smallest, top_value):
    longest = drawn.shape.index(max(drawn.shape))
    spots = []
    for shift in (0, 1):
        where = [jax.random.randint(jax.random.fold_in(key, axis), (), 0, length) for axis, length in enumerate(drawn.shape)]
        where[longest] = (where[longest] + shift) % drawn.shape[longest]
        spots.append(tuple(where))
    return drawn.at[spots[0]].set(smallest).at[spots[1]].set(top_value)


def block_scale(own_key, shape, pieces, low, high):
    gain = 1.0
    for dim, blocks in pieces:
        steps = jax.random.uniform(jax.random.fold_in(jax.random.fold_in(own_key, 6), dim), (blocks,), jnp.float32, low / len(pieces), high / len(pieces))
        gain = gain * jnp.repeat(jnp.exp(steps), shape[dim] // blocks).reshape((-1,) + (1,) * (len(shape) - 1 - dim))
    return gain


def scatter_about(stream_key, dims, width, most, cuts=(), held_as=jnp.bfloat16):
    values = jax.random.normal(stream_key, dims, jnp.float32) * width
    if len(cuts) > 0:
        values = block_scale(stream_key, dims, cuts, -0.22, 0.18) * values
    return jnp.clip(values, min=-most, max=most).astype(held_as)


def setup_inputs(seed: int = 0) -> dict:
    key_of = jax.random.split(jax.random.key(seed), 4)
    return {
        "fluid_temp": scatter_about(key_of[0], (NZ, NY, NX), 1.0, 6.0, ((0, 16), (1, 2))),
        "solid_temp": scatter_about(key_of[1], (2, NX, SY, NZ), 1.0, 6.0, ((1, 16), (3, 2)), jnp.float32),
        "material": with_ends(jax.random.randint(key_of[2], (2, NX, SY, NZ), 0, 4), jax.random.fold_in(key_of[2], 1), 0, 3).astype(jnp.int32),
    }


SIGMA = 0.1
SOLID_STEP = 0.04
HIGHEST = lax.Precision.HIGHEST

def fourier_rows(length, row_ids):
    col_ids = jnp.arange(length, dtype=jnp.int32)[None, :]
    row_ids = row_ids.astype(jnp.int32)[:, None]
    wave_num = (row_ids + 1) // 2
    angles = (wave_num * col_ids % length).astype(jnp.float32) * (2.0 * math.pi / length)
    factor = jnp.where((wave_num == 0) | (2 * wave_num == length), math.sqrt(1.0 / length), math.sqrt(2.0 / length))
    return factor * jnp.where((row_ids % 2 == 1) | (row_ids == 0), jnp.cos(angles), jnp.sin(angles))

def fourier_eigen(length, row_ids):
    wave_num = (row_ids.astype(jnp.int32) + 1) // 2
    return 2.0 - 2.0 * jnp.cos(wave_num.astype(jnp.float32) * (2.0 * math.pi / length))

def sine_table(length):
    row_ids = jnp.arange(length, dtype=jnp.int32)[:, None]
    col_ids = jnp.arange(length, dtype=jnp.int32)[None, :]
    angles = ((row_ids + 1) * (col_ids + 1) % (2 * length + 2)).astype(jnp.float32) * (math.pi / (length + 1))
    return math.sqrt(2.0 / (length + 1)) * jnp.sin(angles)

def sine_eigen(length):
    col_ids = jnp.arange(length, dtype=jnp.int32)
    return 2.0 - 2.0 * jnp.cos((col_ids + 1).astype(jnp.float32) * (math.pi / (length + 1)))

def conductivity(material):
    return jnp.where(material == 0, 0.5, jnp.where(material == 1, 1.0, jnp.where(material == 2, 2.0, 4.0))).astype(jnp.float32)

def harmonic(first, second):
    return 2.0 * first * second / (first + second)

def helmholtz(spectra, span_eigen, wall_vecs, wall_eigen, stream_vecs, stream_eigen):
    coeffs = jnp.einsum('myx,yq->mqx', spectra, wall_vecs, precision=HIGHEST)
    coeffs = jnp.einsum('mqx,px->mqp', coeffs, stream_vecs, precision=HIGHEST)
    coeffs = coeffs / (SIGMA + span_eigen[:, None, None] + wall_eigen[None, :, None] + stream_eigen[None, None, :])
    coeffs = jnp.einsum('mqp,px->mqx', coeffs, stream_vecs, precision=HIGHEST)
    return jnp.einsum('mqx,yq->myx', coeffs, wall_vecs, precision=HIGHEST)

def solid_update(thermal, conduct, wall_flux):
    divergence = jnp.zeros_like(thermal)
    for shift_by, axis_id in ((-1, 1), (1, 1), (-1, 3), (1, 3)):
        divergence = divergence + harmonic(jnp.roll(conduct, shift_by, axis_id), conduct) * (jnp.roll(thermal, shift_by, axis_id) - thermal)
    normal = harmonic(conduct[:, :, 1:, :], conduct[:, :, :-1, :]) * (thermal[:, :, 1:, :] - thermal[:, :, :-1, :])
    divergence = divergence + jnp.pad(normal, ((0, 0), (0, 0), (0, 1), (0, 0))) - jnp.pad(normal, ((0, 0), (0, 0), (1, 0), (0, 0)))
    divergence = divergence.at[:, :, 0, :].add(wall_flux)
    return thermal + SOLID_STEP * divergence

def reference(fluid_temp, solid_temp, material):
    span_ids = jnp.arange(NZ, dtype=jnp.int32)
    span_table = fourier_rows(NZ, span_ids)
    wall_temp = solid_temp[:, :, 0, :]
    wall_hat = jnp.einsum('mz,wxz->wmx', span_table, wall_temp, precision=HIGHEST)
    spectra = jnp.einsum('mz,zyx->myx', span_table, SIGMA * fluid_temp.astype(jnp.float32), precision=HIGHEST)
    spectra = spectra.at[:, 0, :].add(wall_hat[0]).at[:, NY - 1, :].add(wall_hat[1])
    wall_vecs = sine_table(NY)
    wall_eigen = sine_eigen(NY)
    stream_ids = jnp.arange(NX, dtype=jnp.int32)
    stream_vecs = fourier_rows(NX, stream_ids)
    stream_eigen = fourier_eigen(NX, stream_ids)
    span_eigen = fourier_eigen(NZ, span_ids)
    groups = NZ // 8

    def solve_group(packed):
        return helmholtz(packed[0], packed[1], wall_vecs, wall_eigen, stream_vecs, stream_eigen)
    solved = lax.map(solve_group, (spectra.reshape(groups, 8, NY, NX), span_eigen.reshape(groups, 8)))
    fluid_modes = solved.reshape(NZ, NY, NX)
    near_rows = jnp.stack([fluid_modes[:, 0, :], fluid_modes[:, NY - 1, :]])
    wall_flux = jnp.einsum('mz,wmx->wxz', span_table, near_rows, precision=HIGHEST) - wall_temp
    conduct = conductivity(material)
    thermal = solid_temp
    for substep_id in range(SUBSTEPS):
        thermal = solid_update(thermal, conduct, wall_flux)
    return (fluid_modes, thermal)
```

```python
import functools
import math

import jax
import jax.numpy as jnp
import numpy as np
from jax import lax
from jax.experimental import pallas as pl
from jax.experimental.pallas import tpu as pltpu
from jax.sharding import PartitionSpec as P

SUBSTEPS = 4
SIGMA = 0.1
SOLID_STEP = 0.04
HIGHEST = lax.Precision.HIGHEST
LEVELS = 32767.0
BOTH = ("mode", "tile")


def fourier_table(length):
    rows = np.arange(length)[:, None]
    cols = np.arange(length)[None, :]
    wave_num = (rows + 1) // 2
    angles = (wave_num * cols % length) * (2.0 * math.pi / length)
    factor = np.where(
        (wave_num == 0) | (2 * wave_num == length), math.sqrt(1.0 / length), math.sqrt(2.0 / length)
    )
    return factor * np.where((rows % 2 == 1) | (rows == 0), np.cos(angles), np.sin(angles))


def fourier_eigen(length):
    wave_num = (np.arange(length) + 1) // 2
    return 2.0 - 2.0 * np.cos(wave_num * (2.0 * math.pi / length))


def sine_table(length):
    ids = np.arange(length) + 1
    angles = (ids[:, None] * ids[None, :] % (2 * length + 2)) * (math.pi / (length + 1))
    return math.sqrt(2.0 / (length + 1)) * np.sin(angles)


def sine_eigen(length):
    return 2.0 - 2.0 * np.cos((np.arange(length) + 1) * (math.pi / (length + 1)))


def split_table(table):
    high = table.astype(jnp.bfloat16)
    low = (table - high.astype(np.float64)).astype(jnp.bfloat16)
    return np.stack([high, low])


def split(value):
    high = value.astype(jnp.bfloat16)
    return high, (value - high.astype(jnp.float32)).astype(jnp.bfloat16)


def mm(first, second):
    return jnp.dot(first, second, preferred_element_type=jnp.float32)


def table_right(value, table):
    high, low = split(value)
    return mm(high, table[0]) + (mm(low, table[0]) + mm(high, table[1]))


def table_left(table, value):
    high, low = split(value)
    return mm(table[0], high) + (mm(table[0], low) + mm(table[1], high))


def span_kernel(rows_y, width, table_ref, fluid_ref, code_ref, scale_ref):
    lane = lax.broadcasted_iota(jnp.int32, scale_ref.shape, 1)
    scales = jnp.zeros(scale_ref.shape, jnp.float32)
    for row in range(rows_y):
        cols = pl.ds(row * width, width)
        fluid = fluid_ref[:, cols]
        spectra = mm(table_ref[0], fluid) + mm(table_ref[1], fluid)
        top = jnp.maximum(jnp.max(jnp.abs(spectra), axis=1, keepdims=True), 1e-30)
        code_ref[:, cols] = jnp.round(spectra * (LEVELS / top)).astype(jnp.int32).astype(jnp.int16)
        scales = jnp.where(lane == row, top * (1.0 / LEVELS), scales)
    scale_ref[...] = scales


def span_transform(table, fluid, rows_y):
    modes, points = table.shape[1:]
    width = fluid.shape[1]
    block = min(128, modes)
    return pl.pallas_call(
        functools.partial(span_kernel, rows_y, width // rows_y),
        grid=(modes // block,),
        in_specs=[
            pl.BlockSpec((2, block, points), lambda i: (0, i, 0)),
            pl.BlockSpec((points, width), lambda i: (0, 0)),
        ],
        out_specs=[
            pl.BlockSpec((block, width), lambda i: (i, 0)),
            pl.BlockSpec((block, 128), lambda i: (i, 0)),
        ],
        out_shape=[
            jax.ShapeDtypeStruct((modes, width), jnp.int16),
            jax.ShapeDtypeStruct((modes, 128), jnp.float32),
        ],
        compiler_params=pltpu.CompilerParams(vmem_limit_bytes=48 << 20),
        cost_estimate=pl.CostEstimate(
            flops=4 * modes * points * width, bytes_accessed=4 * modes * width, transcendentals=0
        ),
    )(table, fluid)


def helmholtz_kernel(
    spectra_ref, wall_ref, eigen_ref, wall_eigen_ref, into_q, into_p, from_p, from_q, out_ref
):
    spectra = spectra_ref[0]
    row = lax.broadcasted_iota(jnp.int32, spectra.shape, 0)
    spectra = spectra + jnp.where(row == 0, wall_ref[0, 0:1, :], 0.0)
    spectra = spectra + jnp.where(row == spectra.shape[0] - 1, wall_ref[0, 1:2, :], 0.0)
    coeffs = table_right(table_left(into_q, spectra), into_p)
    coeffs = coeffs / (eigen_ref[0] + wall_eigen_ref[...])
    out_ref[0] = table_left(from_q, table_right(coeffs, from_p))


def helmholtz(spectra, wall_hat, eigen, wall_eigen, tables):
    modes, n_y, n_x = spectra.shape
    whole = lambda array: pl.BlockSpec(array.shape, lambda i: (0,) * array.ndim)
    each = lambda array: pl.BlockSpec((1,) + array.shape[1:], lambda i: (i, 0, 0))
    return pl.pallas_call(
        helmholtz_kernel,
        grid=(modes,),
        in_specs=[each(spectra), each(wall_hat), each(eigen), whole(wall_eigen)]
        + [whole(table) for table in tables],
        out_specs=each(spectra),
        out_shape=jax.ShapeDtypeStruct(spectra.shape, jnp.float32),
        compiler_params=pltpu.CompilerParams(vmem_limit_bytes=48 << 20),
        cost_estimate=pl.CostEstimate(
            flops=12 * modes * n_y * n_x * (n_x + n_y),
            bytes_accessed=8 * modes * n_y * n_x,
            transcendentals=0,
        ),
    )(spectra, wall_hat, eigen, wall_eigen, *tables)


def padded(array, axis, dim, width):
    size, length = (lax.axis_size(axis), array.shape[dim])
    up = [(i, (i + 1) % size) for i in range(size)]
    down = [(j, i) for i, j in up]
    last = lax.slice_in_dim(array, length - width, length, axis=dim)
    first = lax.slice_in_dim(array, 0, width, axis=dim)
    return [lax.ppermute(last, axis, up), array, lax.ppermute(first, axis, down)]


def harmonic(first, second):
    return 2.0 * first * second / (first + second)


def conduct_step(thermal, faces, trim):
    face_x, face_y, face_z = faces
    n_x, n_y, n_z = thermal.shape[1:]
    centre = thermal[:, 1:-1, :, 1:-1]
    lo_x, lo_z = trim, trim
    cells_x = slice(lo_x + 1, lo_x + n_x - 1)
    cells_z = slice(lo_z + 1, lo_z + n_z - 1)
    fx = face_x[:, lo_x : lo_x + n_x - 1, :n_y, cells_z]
    fz = face_z[:, cells_x, :n_y, lo_z : lo_z + n_z - 1]
    fy = face_y[:, cells_x, : n_y - 1, cells_z]
    change = fx[:, 1:] * (thermal[:, 2:, :, 1:-1] - centre)
    change = change + fx[:, :-1] * (thermal[:, :-2, :, 1:-1] - centre)
    change = change + fz[..., 1:] * (thermal[:, 1:-1, :, 2:] - centre)
    change = change + fz[..., :-1] * (thermal[:, 1:-1, :, :-2] - centre)
    normal = fy * (centre[:, :, 1:] - centre[:, :, :-1])
    change = (
        change
        + jnp.pad(normal, ((0, 0), (0, 0), (0, 1), (0, 0)))
        - jnp.pad(normal, ((0, 0), (0, 0), (1, 0), (0, 0)))
    )
    return centre + SOLID_STEP * change


def per_device(fluid_temp, solid_temp, material):
    n_mode = lax.axis_size("mode")
    n_tile = lax.axis_size("tile")
    n_dev = n_mode * n_tile
    mode_idx = lax.axis_index("mode")
    tile_idx = lax.axis_index("tile")
    z_rows, y_rows, n_x = fluid_temp.shape
    n_z = z_rows * n_mode
    n_y = y_rows * n_tile
    x_rows = solid_temp.shape[1]
    z_cols = solid_temp.shape[3]
    per_dev = n_z // n_dev
    rows_y = y_rows // n_mode
    halo = SUBSTEPS

    span = fourier_table(n_z)
    span_wide = jnp.asarray(
        np.concatenate([span[:, -halo:], span, span[:, :halo]], axis=1), jnp.float32
    )
    span_wide = lax.dynamic_slice_in_dim(span_wide, tile_idx * z_cols, z_cols + 2 * halo, axis=1)
    span_own = span_wide[:, halo : halo + z_cols]

    blocks = fluid_temp.reshape(z_rows, n_mode, rows_y * n_x).transpose(1, 0, 2)
    fluid = lax.all_to_all(blocks, "mode", split_axis=0, concat_axis=0, tiled=True)
    codes, scales = span_transform(
        jnp.asarray(split_table(SIGMA * span)), fluid.reshape(n_z, rows_y * n_x), rows_y
    )

    wall_part = jnp.einsum(
        "mz,wxz->mwx", span_own, solid_temp[:, :, 0, :], precision=HIGHEST
    ).reshape(n_z, 2 * x_rows)
    small = jnp.concatenate([scales[:, :rows_y], wall_part], axis=1)
    small = lax.all_to_all(small, BOTH, split_axis=0, concat_axis=0, tiled=True)
    codes = lax.all_to_all(codes, BOTH, split_axis=0, concat_axis=0, tiled=True)
    small = small.reshape(n_mode, n_tile, per_dev, rows_y + 2 * x_rows)
    wall_hat = (
        small[..., rows_y:]
        .sum(axis=1)
        .reshape(n_mode, per_dev, 2, x_rows)
        .transpose(1, 2, 0, 3)
        .reshape(per_dev, 2, n_x)
    )
    scales = small[..., :rows_y].reshape(n_dev, per_dev, rows_y, 1)
    spectra = codes.reshape(n_dev, per_dev, rows_y, n_x).astype(jnp.float32) * scales
    spectra = spectra.transpose(1, 0, 2, 3).reshape(per_dev, n_y, n_x)

    arrived = np.arange(n_y).reshape(n_tile, n_mode, rows_y).transpose(1, 0, 2).reshape(n_y)
    sine = sine_table(n_y)
    stream = fourier_table(n_x)
    tables = [
        jnp.asarray(split_table(table)) for table in (sine[arrived].T, stream.T, stream, sine)
    ]
    span_eigen = lax.dynamic_slice_in_dim(
        jnp.asarray(fourier_eigen(n_z), jnp.float32),
        (mode_idx * n_tile + tile_idx) * per_dev,
        per_dev,
    )
    stream_eigen = jnp.asarray(fourier_eigen(n_x), jnp.float32)
    eigen = SIGMA + span_eigen[:, None, None] + stream_eigen[None, None, :]
    wall_eigen = jnp.asarray(sine_eigen(n_y), jnp.float32)[:, None]
    fluid_modes = helmholtz(spectra, wall_hat, eigen, wall_eigen, tables)

    conduct = jnp.where(
        material == 0, 0.5, jnp.where(material == 1, 1.0, jnp.where(material == 2, 2.0, 4.0))
    ).astype(jnp.float32)
    both = jnp.concatenate(padded(jnp.stack([solid_temp, conduct]), "mode", 2, halo), axis=2)
    before, both, after = padded(both, "tile", 4, halo)
    both = jnp.concatenate([before, both, after], axis=4)
    start, conduct = both[0], both[1]
    faces = (
        harmonic(conduct[:, 1:], conduct[:, :-1]),
        harmonic(conduct[:, :, 1:], conduct[:, :, :-1]),
        harmonic(conduct[..., 1:], conduct[..., :-1]),
    )
    thermal = start
    for trim in range(SUBSTEPS):
        thermal = conduct_step(thermal, faces, trim)

    near = jnp.stack([fluid_modes[:, 0, :], fluid_modes[:, n_y - 1, :]], axis=1)
    near = jnp.concatenate([near[..., -halo:], near, near[..., :halo]], axis=2)
    span_x = x_rows + 2 * halo
    near = jnp.stack([near[..., b * x_rows : b * x_rows + span_x] for b in range(n_mode)])
    near = jnp.broadcast_to(
        near.reshape(n_mode, 1, per_dev, 2 * span_x), (n_mode, n_tile, per_dev, 2 * span_x)
    ).reshape(n_z, 2 * span_x)
    near = lax.all_to_all(near, BOTH, split_axis=0, concat_axis=0, tiled=True)
    wall_flux = jnp.einsum(
        "mwx,mz->wxz", near.reshape(n_z, 2, span_x), span_wide, precision=HIGHEST
    )
    wall_flux = SOLID_STEP * (wall_flux - start[:, :, 0, :])
    added = jnp.pad(wall_flux[:, :, None, :], ((0, 0), (0, 0), (0, SUBSTEPS - 1), (0, 0)))
    source = added
    added = added[:, 1:-1, :, 1:-1]
    for trim in range(1, SUBSTEPS):
        ring = slice(trim + 1, -trim - 1)
        added = conduct_step(added, faces, trim) + source[:, ring, :, ring]
    thermal = jnp.concatenate(
        [thermal[:, :, :SUBSTEPS] + added, thermal[:, :, SUBSTEPS:]], axis=2
    )
    return (fluid_modes, thermal)


def solution(mesh):
    placed = (P("mode", "tile", None), P(None, "mode", None, "tile"), P(None, "mode", None, "tile"))
    return jax.shard_map(
        per_device,
        mesh=mesh,
        in_specs=placed,
        out_specs=(P(BOTH, None, None), P(None, "mode", None, "tile")),
        check_vma=False,
    )
```

```python
import functools
import math

import jax
import jax.numpy as jnp
import numpy as np
from jax import lax
from jax.experimental import pallas as pl
from jax.experimental.pallas import tpu as pltpu
from jax.sharding import PartitionSpec as P

SUBSTEPS = 4
SIGMA = 0.1
SOLID_STEP = 0.04
HIGHEST = lax.Precision.HIGHEST
LEVELS = 32767.0
BOTH = ("mode", "tile")


def fourier_table(length):
    rows = np.arange(length)[:, None]
    cols = np.arange(length)[None, :]
    wave_num = (rows + 1) // 2
    angles = (wave_num * cols % length) * (2.0 * math.pi / length)
    factor = np.where(
        (wave_num == 0) | (2 * wave_num == length), math.sqrt(1.0 / length), math.sqrt(2.0 / length)
    )
    return factor * np.where((rows % 2 == 1) | (rows == 0), np.cos(angles), np.sin(angles))


def fourier_eigen(length):
    wave_num = (np.arange(length) + 1) // 2
    return 2.0 - 2.0 * np.cos(wave_num * (2.0 * math.pi / length))


def sine_table(length):
    ids = np.arange(length) + 1
    angles = (ids[:, None] * ids[None, :] % (2 * length + 2)) * (math.pi / (length + 1))
    return math.sqrt(2.0 / (length + 1)) * np.sin(angles)


def sine_eigen(length):
    return 2.0 - 2.0 * np.cos((np.arange(length) + 1) * (math.pi / (length + 1)))


def split_table(table):
    high = table.astype(jnp.bfloat16)
    low = (table - high.astype(np.float64)).astype(jnp.bfloat16)
    return np.stack([high, low])


def split(value):
    high = value.astype(jnp.bfloat16)
    return high, (value - high.astype(jnp.float32)).astype(jnp.bfloat16)


def mm(first, second):
    return jnp.dot(first, second, preferred_element_type=jnp.float32)


def table_right(value, table):
    high, low = split(value)
    return mm(high, table[0]) + (mm(low, table[0]) + mm(high, table[1]))


def table_left(table, value):
    high, low = split(value)
    return mm(table[0], high) + (mm(table[0], low) + mm(table[1], high))


def span_kernel(rows_y, width, table_ref, fluid_ref, code_ref, scale_ref):
    lane = lax.broadcasted_iota(jnp.int32, scale_ref.shape, 1)
    scales = jnp.zeros(scale_ref.shape, jnp.float32)
    for row in range(rows_y):
        cols = pl.ds(row * width, width)
        fluid = fluid_ref[:, cols]
        spectra = mm(table_ref[0], fluid) + mm(table_ref[1], fluid)
        top = jnp.maximum(jnp.max(jnp.abs(spectra), axis=1, keepdims=True), 1e-30)
        code_ref[:, cols] = jnp.round(spectra * (LEVELS / top)).astype(jnp.int32).astype(jnp.int16)
        scales = jnp.where(lane == row, top * (1.0 / LEVELS), scales)
    scale_ref[...] = scales


def span_transform(table, fluid, rows_y):
    modes, points = table.shape[1:]
    width = fluid.shape[1]
    block = min(128, modes)
    return pl.pallas_call(
        functools.partial(span_kernel, rows_y, width // rows_y),
        grid=(modes // block,),
        in_specs=[
            pl.BlockSpec((2, block, points), lambda i: (0, i, 0)),
            pl.BlockSpec((points, width), lambda i: (0, 0)),
        ],
        out_specs=[
            pl.BlockSpec((block, width), lambda i: (i, 0)),
            pl.BlockSpec((block, 128), lambda i: (i, 0)),
        ],
        out_shape=[
            jax.ShapeDtypeStruct((modes, width), jnp.int16),
            jax.ShapeDtypeStruct((modes, 128), jnp.float32),
        ],
        compiler_params=pltpu.CompilerParams(vmem_limit_bytes=48 << 20),
        cost_estimate=pl.CostEstimate(
            flops=4 * modes * points * width, bytes_accessed=4 * modes * width, transcendentals=0
        ),
    )(table, fluid)


def helmholtz_kernel(
    spectra_ref, wall_ref, eigen_ref, wall_eigen_ref, into_q, into_p, from_p, from_q, out_ref
):
    spectra = spectra_ref[0]
    row = lax.broadcasted_iota(jnp.int32, spectra.shape, 0)
    spectra = spectra + jnp.where(row == 0, wall_ref[0, 0:1, :], 0.0)
    spectra = spectra + jnp.where(row == spectra.shape[0] - 1, wall_ref[0, 1:2, :], 0.0)
    coeffs = table_right(table_left(into_q, spectra), into_p)
    coeffs = coeffs / (eigen_ref[0] + wall_eigen_ref[...])
    out_ref[0] = table_left(from_q, table_right(coeffs, from_p))


def helmholtz(spectra, wall_hat, eigen, wall_eigen, tables):
    modes, n_y, n_x = spectra.shape
    whole = lambda array: pl.BlockSpec(array.shape, lambda i: (0,) * array.ndim)
    each = lambda array: pl.BlockSpec((1,) + array.shape[1:], lambda i: (i, 0, 0))
    return pl.pallas_call(
        helmholtz_kernel,
        grid=(modes,),
        in_specs=[each(spectra), each(wall_hat), each(eigen), whole(wall_eigen)]
        + [whole(table) for table in tables],
        out_specs=each(spectra),
        out_shape=jax.ShapeDtypeStruct(spectra.shape, jnp.float32),
        compiler_params=pltpu.CompilerParams(vmem_limit_bytes=48 << 20),
        cost_estimate=pl.CostEstimate(
            flops=12 * modes * n_y * n_x * (n_x + n_y),
            bytes_accessed=8 * modes * n_y * n_x,
            transcendentals=0,
        ),
    )(spectra, wall_hat, eigen, wall_eigen, *tables)


def padded(array, axis, dim, width):
    size, length = (lax.axis_size(axis), array.shape[dim])
    up = [(i, (i + 1) % size) for i in range(size)]
    down = [(j, i) for i, j in up]
    last = lax.slice_in_dim(array, length - width, length, axis=dim)
    first = lax.slice_in_dim(array, 0, width, axis=dim)
    return [lax.ppermute(last, axis, up), array, lax.ppermute(first, axis, down)]


def harmonic(first, second):
    return 2.0 * first * second / (first + second)


def conduct_step(thermal, faces, trim):
    face_x, face_y, face_z = faces
    n_x, n_y, n_z = thermal.shape[1:]
    centre = thermal[:, 1:-1, :, 1:-1]
    lo_x, lo_z = trim, trim
    cells_x = slice(lo_x + 1, lo_x + n_x - 1)
    cells_z = slice(lo_z + 1, lo_z + n_z - 1)
    fx = face_x[:, lo_x : lo_x + n_x - 1, :n_y, cells_z]
    fz = face_z[:, cells_x, :n_y, lo_z : lo_z + n_z - 1]
    fy = face_y[:, cells_x, : n_y - 1, cells_z]
    change = fx[:, 1:] * (thermal[:, 2:, :, 1:-1] - centre)
    change = change + fx[:, :-1] * (thermal[:, :-2, :, 1:-1] - centre)
    change = change + fz[..., 1:] * (thermal[:, 1:-1, :, 2:] - centre)
    change = change + fz[..., :-1] * (thermal[:, 1:-1, :, :-2] - centre)
    normal = fy * (centre[:, :, 1:] - centre[:, :, :-1])
    change = (
        change
        + jnp.pad(normal, ((0, 0), (0, 0), (0, 1), (0, 0)))
        - jnp.pad(normal, ((0, 0), (0, 0), (1, 0), (0, 0)))
    )
    return centre + SOLID_STEP * change


def conduct_kernel(thermal_ref, conduct_ref, out_ref, held, face_x, face_y, face_z):
    planes, n_y, n_z = held.shape
    n_out = out_ref.shape[3]
    row = lax.broadcasted_iota(jnp.int32, (n_y, n_z), 0)

    def set_faces(x, carry):
        cond = conduct_ref[0, x]
        face_z[x] = SOLID_STEP * harmonic(pltpu.roll(cond, n_z - 1, 1), cond)
        normal = SOLID_STEP * harmonic(pltpu.roll(cond, n_y - 1, 0), cond)
        face_y[x] = jnp.where(row == n_y - 1, 0.0, normal)
        ahead = conduct_ref[0, jnp.minimum(x + 1, planes - 1)]
        face_x[x] = SOLID_STEP * harmonic(ahead, cond)
        return carry

    lax.fori_loop(0, planes, set_faces, 0)
    for step in range(1, SUBSTEPS + 1):
        old = thermal_ref.at[0] if step == 1 else held

        def plane(x, behind):
            here = old[x]
            ahead = face_x[x] * (old[x + 1] - here)
            span = face_z[x] * (pltpu.roll(here, n_z - 1, 1) - here)
            normal = face_y[x] * (pltpu.roll(here, n_y - 1, 0) - here)
            change = (ahead - behind) + (span - pltpu.roll(span, 1, 1))
            change = change + (normal - pltpu.roll(normal, 1, 0))
            if step == SUBSTEPS:
                out_ref[0, x - SUBSTEPS] = (here + change)[:, :n_out]
            else:
                held[x] = here + change
            return ahead

        first = face_x[step - 1] * (old[step] - old[step - 1])
        lax.fori_loop(step, planes - step, plane, first)


def conduct_walls(thermal, conduct, z_cols):
    walls, planes, n_y, n_z = thermal.shape
    rows = planes - 2 * SUBSTEPS
    block = pl.BlockSpec(
        (1, planes, n_y, n_z), lambda w: (w, 0, 0, 0), pipeline_mode=pl.Buffered(1)
    )
    return pl.pallas_call(
        conduct_kernel,
        grid=(walls,),
        in_specs=[block, block],
        out_specs=pl.BlockSpec(
            (1, rows, n_y, z_cols), lambda w: (w, 0, 0, 0), pipeline_mode=pl.Buffered(1)
        ),
        out_shape=jax.ShapeDtypeStruct((walls, rows, n_y, z_cols), jnp.float32),
        scratch_shapes=[pltpu.VMEM((planes, n_y, n_z), jnp.float32) for _ in range(4)],
        compiler_params=pltpu.CompilerParams(vmem_limit_bytes=54 << 20),
        cost_estimate=pl.CostEstimate(
            flops=80 * thermal.size * SUBSTEPS, bytes_accessed=12 * thermal.size, transcendentals=0
        ),
    )(thermal, conduct)


def per_device(fluid_temp, solid_temp, material):
    n_mode = lax.axis_size("mode")
    n_tile = lax.axis_size("tile")
    n_dev = n_mode * n_tile
    mode_idx = lax.axis_index("mode")
    tile_idx = lax.axis_index("tile")
    z_rows, y_rows, n_x = fluid_temp.shape
    n_z = z_rows * n_mode
    n_y = y_rows * n_tile
    x_rows = solid_temp.shape[1]
    z_cols = solid_temp.shape[3]
    per_dev = n_z // n_dev
    rows_y = y_rows // n_mode
    halo = SUBSTEPS

    span = fourier_table(n_z)
    span_wide = jnp.asarray(
        np.concatenate([span[:, -halo:], span, span[:, :halo]], axis=1), jnp.float32
    )
    span_wide = lax.dynamic_slice_in_dim(span_wide, tile_idx * z_cols, z_cols + 2 * halo, axis=1)
    span_own = span_wide[:, halo : halo + z_cols]

    blocks = fluid_temp.reshape(z_rows, n_mode, rows_y * n_x).transpose(1, 0, 2)
    fluid = lax.all_to_all(blocks, "mode", split_axis=0, concat_axis=0, tiled=True)
    codes, scales = span_transform(
        jnp.asarray(split_table(SIGMA * span)), fluid.reshape(n_z, rows_y * n_x), rows_y
    )

    wall_part = jnp.einsum(
        "mz,wxz->mwx", span_own, solid_temp[:, :, 0, :], precision=HIGHEST
    ).reshape(n_z, 2 * x_rows)
    small = jnp.concatenate([scales[:, :rows_y], wall_part], axis=1)
    small = lax.all_to_all(small, BOTH, split_axis=0, concat_axis=0, tiled=True)
    codes = lax.all_to_all(codes, BOTH, split_axis=0, concat_axis=0, tiled=True)
    small = small.reshape(n_mode, n_tile, per_dev, rows_y + 2 * x_rows)
    wall_hat = (
        small[..., rows_y:]
        .sum(axis=1)
        .reshape(n_mode, per_dev, 2, x_rows)
        .transpose(1, 2, 0, 3)
        .reshape(per_dev, 2, n_x)
    )
    scales = small[..., :rows_y].reshape(n_dev, per_dev, rows_y, 1)
    spectra = codes.reshape(n_dev, per_dev, rows_y, n_x).astype(jnp.float32) * scales
    spectra = spectra.transpose(1, 0, 2, 3).reshape(per_dev, n_y, n_x)

    arrived = np.arange(n_y).reshape(n_tile, n_mode, rows_y).transpose(1, 0, 2).reshape(n_y)
    sine = sine_table(n_y)
    stream = fourier_table(n_x)
    tables = [
        jnp.asarray(split_table(table)) for table in (sine[arrived].T, stream.T, stream, sine)
    ]
    span_eigen = lax.dynamic_slice_in_dim(
        jnp.asarray(fourier_eigen(n_z), jnp.float32),
        (mode_idx * n_tile + tile_idx) * per_dev,
        per_dev,
    )
    stream_eigen = jnp.asarray(fourier_eigen(n_x), jnp.float32)
    eigen = SIGMA + span_eigen[:, None, None] + stream_eigen[None, None, :]
    wall_eigen = jnp.asarray(sine_eigen(n_y), jnp.float32)[:, None]
    fluid_modes = helmholtz(spectra, wall_hat, eigen, wall_eigen, tables)

    conduct = jnp.where(
        material == 0, 0.5, jnp.where(material == 1, 1.0, jnp.where(material == 2, 2.0, 4.0))
    ).astype(jnp.float32)
    both = jnp.concatenate(padded(jnp.stack([solid_temp, conduct]), "mode", 2, halo), axis=2)
    before, both, after = padded(both, "tile", 4, halo)
    filling = jnp.ones(both.shape[:4] + (128 - 2 * halo,), jnp.float32)
    both = jnp.concatenate([both, after, filling, before], axis=4)
    thermal = conduct_walls(both[0], both[1], z_cols)
    slab = both[:, :, :, :SUBSTEPS]
    slab = jnp.concatenate([slab[..., -halo:], slab[..., : z_cols + halo]], axis=4)
    start, conduct = slab[0], slab[1]
    faces = (
        harmonic(conduct[:, 1:], conduct[:, :-1]),
        harmonic(conduct[:, :, 1:], conduct[:, :, :-1]),
        harmonic(conduct[..., 1:], conduct[..., :-1]),
    )

    near = jnp.stack([fluid_modes[:, 0, :], fluid_modes[:, n_y - 1, :]], axis=1)
    near = jnp.concatenate([near[..., -halo:], near, near[..., :halo]], axis=2)
    span_x = x_rows + 2 * halo
    near = jnp.stack([near[..., b * x_rows : b * x_rows + span_x] for b in range(n_mode)])
    near = jnp.broadcast_to(
        near.reshape(n_mode, 1, per_dev, 2 * span_x), (n_mode, n_tile, per_dev, 2 * span_x)
    ).reshape(n_z, 2 * span_x)
    near = lax.all_to_all(near, BOTH, split_axis=0, concat_axis=0, tiled=True)
    wall_flux = jnp.einsum(
        "mwx,mz->wxz", near.reshape(n_z, 2, span_x), span_wide, precision=HIGHEST
    )
    wall_flux = SOLID_STEP * (wall_flux - start[:, :, 0, :])
    added = jnp.pad(wall_flux[:, :, None, :], ((0, 0), (0, 0), (0, SUBSTEPS - 1), (0, 0)))
    source = added
    added = added[:, 1:-1, :, 1:-1]
    for trim in range(1, SUBSTEPS):
        ring = slice(trim + 1, -trim - 1)
        added = conduct_step(added, faces, trim) + source[:, ring, :, ring]
    thermal = jnp.concatenate(
        [thermal[:, :, :SUBSTEPS] + added, thermal[:, :, SUBSTEPS:]], axis=2
    )
    return (fluid_modes, thermal)


def solution(mesh):
    placed = (P("mode", "tile", None), P(None, "mode", None, "tile"), P(None, "mode", None, "tile"))
    return jax.shard_map(
        per_device,
        mesh=mesh,
        in_specs=placed,
        out_specs=(P(BOTH, None, None), P(None, "mode", None, "tile")),
        check_vma=False,
    )
```

```python
import functools
import math

import jax
import jax.numpy as jnp
import numpy as np
from jax import lax
from jax.experimental import pallas as pl
from jax.experimental.pallas import tpu as pltpu
from jax.sharding import PartitionSpec as P

SUBSTEPS = 4
SIGMA = 0.1
SOLID_STEP = 0.04
HIGHEST = lax.Precision.HIGHEST
LEVELS = 32767.0
BOTH = ("mode", "tile")


def fourier_table(length):
    rows = np.arange(length)[:, None]
    cols = np.arange(length)[None, :]
    wave_num = (rows + 1) // 2
    angles = (wave_num * cols % length) * (2.0 * math.pi / length)
    factor = np.where(
        (wave_num == 0) | (2 * wave_num == length), math.sqrt(1.0 / length), math.sqrt(2.0 / length)
    )
    return factor * np.where((rows % 2 == 1) | (rows == 0), np.cos(angles), np.sin(angles))


def fourier_eigen(length):
    wave_num = (np.arange(length) + 1) // 2
    return 2.0 - 2.0 * np.cos(wave_num * (2.0 * math.pi / length))


def sine_table(length):
    ids = np.arange(length) + 1
    angles = (ids[:, None] * ids[None, :] % (2 * length + 2)) * (math.pi / (length + 1))
    return math.sqrt(2.0 / (length + 1)) * np.sin(angles)


def sine_eigen(length):
    return 2.0 - 2.0 * np.cos((np.arange(length) + 1) * (math.pi / (length + 1)))


def split_table(table):
    high = table.astype(jnp.bfloat16)
    low = (table - high.astype(np.float64)).astype(jnp.bfloat16)
    return np.stack([high, low])


def split(value):
    high = value.astype(jnp.bfloat16)
    return high, (value - high.astype(jnp.float32)).astype(jnp.bfloat16)


def mm(first, second):
    return jnp.dot(first, second, preferred_element_type=jnp.float32)


def table_right(value, table):
    high, low = split(value)
    return mm(high, table[0]) + (mm(low, table[0]) + mm(high, table[1]))


def table_left(table, value):
    high, low = split(value)
    return mm(table[0], high) + (mm(table[0], low) + mm(table[1], high))


def span_kernel(rows_y, width, table_ref, fluid_ref, code_ref, scale_ref):
    lane = lax.broadcasted_iota(jnp.int32, scale_ref.shape, 1)
    scales = jnp.zeros(scale_ref.shape, jnp.float32)
    for row in range(rows_y):
        cols = pl.ds(row * width, width)
        fluid = fluid_ref[:, cols]
        spectra = mm(table_ref[0], fluid) + mm(table_ref[1], fluid)
        top = jnp.maximum(jnp.max(jnp.abs(spectra), axis=1, keepdims=True), 1e-30)
        code_ref[:, cols] = jnp.round(spectra * (LEVELS / top)).astype(jnp.int32).astype(jnp.int16)
        scales = jnp.where(lane == row, top * (1.0 / LEVELS), scales)
    scale_ref[...] = scales


def span_transform(table, fluid, rows_y):
    modes, points = table.shape[1:]
    width = fluid.shape[1]
    block = min(128, modes)
    return pl.pallas_call(
        functools.partial(span_kernel, rows_y, width // rows_y),
        grid=(modes // block,),
        in_specs=[
            pl.BlockSpec((2, block, points), lambda i: (0, i, 0)),
            pl.BlockSpec((points, width), lambda i: (0, 0)),
        ],
        out_specs=[
            pl.BlockSpec((block, width), lambda i: (i, 0)),
            pl.BlockSpec((block, 128), lambda i: (i, 0)),
        ],
        out_shape=[
            jax.ShapeDtypeStruct((modes, width), jnp.int16),
            jax.ShapeDtypeStruct((modes, 128), jnp.float32),
        ],
        compiler_params=pltpu.CompilerParams(vmem_limit_bytes=48 << 20),
        cost_estimate=pl.CostEstimate(
            flops=4 * modes * points * width, bytes_accessed=4 * modes * width, transcendentals=0
        ),
    )(table, fluid)


def helmholtz_kernel(
    spectra_ref, wall_ref, eigen_ref, wall_eigen_ref, into_q, into_p, from_p, from_q, out_ref
):
    spectra = spectra_ref[0]
    row = lax.broadcasted_iota(jnp.int32, spectra.shape, 0)
    spectra = spectra + jnp.where(row == 0, wall_ref[0, 0:1, :], 0.0)
    spectra = spectra + jnp.where(row == spectra.shape[0] - 1, wall_ref[0, 1:2, :], 0.0)
    coeffs = table_right(table_left(into_q, spectra), into_p)
    coeffs = coeffs / (eigen_ref[0] + wall_eigen_ref[...])
    out_ref[0] = table_left(from_q, table_right(coeffs, from_p))


def helmholtz(spectra, wall_hat, eigen, wall_eigen, tables):
    modes, n_y, n_x = spectra.shape
    whole = lambda array: pl.BlockSpec(array.shape, lambda i: (0,) * array.ndim)
    each = lambda array: pl.BlockSpec((1,) + array.shape[1:], lambda i: (i, 0, 0))
    return pl.pallas_call(
        helmholtz_kernel,
        grid=(modes,),
        in_specs=[each(spectra), each(wall_hat), each(eigen), whole(wall_eigen)]
        + [whole(table) for table in tables],
        out_specs=each(spectra),
        out_shape=jax.ShapeDtypeStruct(spectra.shape, jnp.float32),
        compiler_params=pltpu.CompilerParams(vmem_limit_bytes=48 << 20),
        cost_estimate=pl.CostEstimate(
            flops=12 * modes * n_y * n_x * (n_x + n_y),
            bytes_accessed=8 * modes * n_y * n_x,
            transcendentals=0,
        ),
    )(spectra, wall_hat, eigen, wall_eigen, *tables)


def padded(array, axis, dim, width):
    size, length = (lax.axis_size(axis), array.shape[dim])
    up = [(i, (i + 1) % size) for i in range(size)]
    down = [(j, i) for i, j in up]
    last = lax.slice_in_dim(array, length - width, length, axis=dim)
    first = lax.slice_in_dim(array, 0, width, axis=dim)
    return [lax.ppermute(last, axis, up), array, lax.ppermute(first, axis, down)]


def harmonic(first, second):
    return 2.0 * first * second / (first + second)


def conduct_step(thermal, faces, trim):
    face_x, face_y, face_z = faces
    n_x, n_y, n_z = thermal.shape[1:]
    centre = thermal[:, 1:-1, :, 1:-1]
    lo_x, lo_z = trim, trim
    cells_x = slice(lo_x + 1, lo_x + n_x - 1)
    cells_z = slice(lo_z + 1, lo_z + n_z - 1)
    fx = face_x[:, lo_x : lo_x + n_x - 1, :n_y, cells_z]
    fz = face_z[:, cells_x, :n_y, lo_z : lo_z + n_z - 1]
    fy = face_y[:, cells_x, : n_y - 1, cells_z]
    change = fx[:, 1:] * (thermal[:, 2:, :, 1:-1] - centre)
    change = change + fx[:, :-1] * (thermal[:, :-2, :, 1:-1] - centre)
    change = change + fz[..., 1:] * (thermal[:, 1:-1, :, 2:] - centre)
    change = change + fz[..., :-1] * (thermal[:, 1:-1, :, :-2] - centre)
    normal = fy * (centre[:, :, 1:] - centre[:, :, :-1])
    change = (
        change
        + jnp.pad(normal, ((0, 0), (0, 0), (0, 1), (0, 0)))
        - jnp.pad(normal, ((0, 0), (0, 0), (1, 0), (0, 0)))
    )
    return centre + SOLID_STEP * change


def conduct_kernel(thermal_ref, conduct_ref, out_ref, held, face_x, face_y, face_z):
    planes, n_y, n_z = held.shape
    n_out = out_ref.shape[3]
    row = lax.broadcasted_iota(jnp.int32, (n_y, n_z), 0)

    def set_faces(x, carry):
        cond = conduct_ref[0, x]
        face_z[x] = SOLID_STEP * harmonic(pltpu.roll(cond, n_z - 1, 1), cond)
        normal = SOLID_STEP * harmonic(pltpu.roll(cond, n_y - 1, 0), cond)
        face_y[x] = jnp.where(row == n_y - 1, 0.0, normal)
        ahead = conduct_ref[0, jnp.minimum(x + 1, planes - 1)]
        face_x[x] = SOLID_STEP * harmonic(ahead, cond)
        return carry

    lax.fori_loop(0, planes, set_faces, 0)
    for step in range(1, SUBSTEPS + 1):
        old = thermal_ref.at[0] if step == 1 else held

        def plane(x, behind):
            here = old[x]
            ahead = face_x[x] * (old[x + 1] - here)
            span = face_z[x] * (pltpu.roll(here, n_z - 1, 1) - here)
            normal = face_y[x] * (pltpu.roll(here, n_y - 1, 0) - here)
            change = (ahead - behind) + (span - pltpu.roll(span, 1, 1))
            change = change + (normal - pltpu.roll(normal, 1, 0))
            if step == SUBSTEPS:
                out_ref[0, x - SUBSTEPS] = (here + change)[:, :n_out]
            else:
                held[x] = here + change
            return ahead

        first = face_x[step - 1] * (old[step] - old[step - 1])
        lax.fori_loop(step, planes - step, plane, first)


def conduct_walls(thermal, conduct, z_cols):
    walls, planes, n_y, n_z = thermal.shape
    rows = planes - 2 * SUBSTEPS
    block = pl.BlockSpec(
        (1, planes, n_y, n_z), lambda w: (w, 0, 0, 0), pipeline_mode=pl.Buffered(1)
    )
    return pl.pallas_call(
        conduct_kernel,
        grid=(walls,),
        in_specs=[block, block],
        out_specs=pl.BlockSpec(
            (1, rows, n_y, z_cols), lambda w: (w, 0, 0, 0), pipeline_mode=pl.Buffered(1)
        ),
        out_shape=jax.ShapeDtypeStruct((walls, rows, n_y, z_cols), jnp.float32),
        scratch_shapes=[pltpu.VMEM((planes, n_y, n_z), jnp.float32) for _ in range(4)],
        compiler_params=pltpu.CompilerParams(vmem_limit_bytes=54 << 20),
        cost_estimate=pl.CostEstimate(
            flops=80 * thermal.size * SUBSTEPS, bytes_accessed=12 * thermal.size, transcendentals=0
        ),
    )(thermal, conduct)


def per_device(fluid_temp, solid_temp, material):
    n_mode = lax.axis_size("mode")
    n_tile = lax.axis_size("tile")
    n_dev = n_mode * n_tile
    mode_idx = lax.axis_index("mode")
    tile_idx = lax.axis_index("tile")
    z_rows, y_rows, n_x = fluid_temp.shape
    n_z = z_rows * n_mode
    n_y = y_rows * n_tile
    x_rows = solid_temp.shape[1]
    z_cols = solid_temp.shape[3]
    per_dev = n_z // n_dev
    rows_y = y_rows // n_mode
    halo = SUBSTEPS

    span = fourier_table(n_z)
    span_wide = jnp.asarray(
        np.concatenate([span[:, -halo:], span, span[:, :halo]], axis=1), jnp.float32
    )
    span_wide = lax.dynamic_slice_in_dim(span_wide, tile_idx * z_cols, z_cols + 2 * halo, axis=1)
    span_own = span_wide[:, halo : halo + z_cols]

    blocks = fluid_temp.reshape(z_rows, n_mode, rows_y * n_x).transpose(1, 0, 2)
    conduct = jnp.where(
        material == 0, 0.5, jnp.where(material == 1, 1.0, jnp.where(material == 2, 2.0, 4.0))
    ).astype(jnp.float32)
    both = jnp.concatenate(padded(jnp.stack([solid_temp, conduct]), "mode", 2, halo), axis=2)
    before, both, after = padded(both, "tile", 4, halo)
    blocks, before, both, after = lax.optimization_barrier((blocks, before, both, after))
    fluid = lax.all_to_all(blocks, "mode", split_axis=0, concat_axis=0, tiled=True)
    codes, scales = span_transform(
        jnp.asarray(split_table(SIGMA * span)), fluid.reshape(n_z, rows_y * n_x), rows_y
    )

    wall_part = jnp.einsum(
        "mz,wxz->mwx", span_own, solid_temp[:, :, 0, :], precision=HIGHEST
    ).reshape(n_z, 2 * x_rows)
    small = jnp.concatenate([scales[:, :rows_y], wall_part], axis=1)
    small = lax.all_to_all(small, BOTH, split_axis=0, concat_axis=0, tiled=True)
    codes = lax.all_to_all(codes, BOTH, split_axis=0, concat_axis=0, tiled=True)
    small = small.reshape(n_mode, n_tile, per_dev, rows_y + 2 * x_rows)
    wall_hat = (
        small[..., rows_y:]
        .sum(axis=1)
        .reshape(n_mode, per_dev, 2, x_rows)
        .transpose(1, 2, 0, 3)
        .reshape(per_dev, 2, n_x)
    )
    scales = small[..., :rows_y].reshape(n_dev, per_dev, rows_y, 1)
    spectra = codes.reshape(n_dev, per_dev, rows_y, n_x).astype(jnp.float32) * scales
    spectra = spectra.transpose(1, 0, 2, 3).reshape(per_dev, n_y, n_x)

    arrived = np.arange(n_y).reshape(n_tile, n_mode, rows_y).transpose(1, 0, 2).reshape(n_y)
    sine = sine_table(n_y)
    stream = fourier_table(n_x)
    tables = [
        jnp.asarray(split_table(table)) for table in (sine[arrived].T, stream.T, stream, sine)
    ]
    span_eigen = lax.dynamic_slice_in_dim(
        jnp.asarray(fourier_eigen(n_z), jnp.float32),
        (mode_idx * n_tile + tile_idx) * per_dev,
        per_dev,
    )
    stream_eigen = jnp.asarray(fourier_eigen(n_x), jnp.float32)
    eigen = SIGMA + span_eigen[:, None, None] + stream_eigen[None, None, :]
    wall_eigen = jnp.asarray(sine_eigen(n_y), jnp.float32)[:, None]
    fluid_modes = helmholtz(spectra, wall_hat, eigen, wall_eigen, tables)

    filling = jnp.ones(both.shape[:4] + (128 - 2 * halo,), jnp.float32)
    both = jnp.concatenate([both, after, filling, before], axis=4)
    thermal = conduct_walls(both[0], both[1], z_cols)
    slab = both[:, :, :, :SUBSTEPS]
    slab = jnp.concatenate([slab[..., -halo:], slab[..., : z_cols + halo]], axis=4)
    start, conduct = slab[0], slab[1]
    faces = (
        harmonic(conduct[:, 1:], conduct[:, :-1]),
        harmonic(conduct[:, :, 1:], conduct[:, :, :-1]),
        harmonic(conduct[..., 1:], conduct[..., :-1]),
    )

    near = jnp.stack([fluid_modes[:, 0, :], fluid_modes[:, n_y - 1, :]], axis=1)
    near = jnp.concatenate([near[..., -halo:], near, near[..., :halo]], axis=2)
    span_x = x_rows + 2 * halo
    near = jnp.stack([near[..., b * x_rows : b * x_rows + span_x] for b in range(n_mode)])
    near = jnp.broadcast_to(
        near.reshape(n_mode, 1, per_dev, 2 * span_x), (n_mode, n_tile, per_dev, 2 * span_x)
    ).reshape(n_z, 2 * span_x)
    near = lax.all_to_all(near, BOTH, split_axis=0, concat_axis=0, tiled=True)
    wall_flux = jnp.einsum(
        "mwx,mz->wxz", near.reshape(n_z, 2, span_x), span_wide, precision=HIGHEST
    )
    wall_flux = SOLID_STEP * (wall_flux - start[:, :, 0, :])
    added = jnp.pad(wall_flux[:, :, None, :], ((0, 0), (0, 0), (0, SUBSTEPS - 1), (0, 0)))
    source = added
    added = added[:, 1:-1, :, 1:-1]
    for trim in range(1, SUBSTEPS):
        ring = slice(trim + 1, -trim - 1)
        added = conduct_step(added, faces, trim) + source[:, ring, :, ring]
    thermal = jnp.concatenate(
        [thermal[:, :, :SUBSTEPS] + added, thermal[:, :, SUBSTEPS:]], axis=2
    )
    return (fluid_modes, thermal)


def solution(mesh):
    placed = (P("mode", "tile", None), P(None, "mode", None, "tile"), P(None, "mode", None, "tile"))
    return jax.shard_map(
        per_device,
        mesh=mesh,
        in_specs=placed,
        out_specs=(P(BOTH, None, None), P(None, "mode", None, "tile")),
        check_vma=False,
    )
```
